512 devices in a mesh: expert: 64 (over x, z), tensor: 8 (over y, core).
Axes of the slice: x: 4, y: 4, z: 16, core: 2. Of those that a mesh axis runs over, the one named last changes fastest.
Arguments:
- context: bfloat16 [2048, 3072], P('expert', 'tensor'), may hold values from -6 to 6
- out_weight: bfloat16 [3072, 3072], P('tensor', 'expert'), may hold values from -0.109375 to 0.109375
- residual: bfloat16 [2048, 3072], P(('expert', 'tensor')), may hold values from -6 to 6
- norm_gain: bfloat16 [3072], replicated, may hold values from 0.099609375 to 1.8984375
- router_weight: bfloat16 [3072, 16], replicated, may hold values from -0.109375 to 0.109375
- gate_weight: bfloat16 [3072, 131072], P(None, ('expert', 'tensor')), may hold values from -0.109375 to 0.109375
- up_weight: bfloat16 [3072, 131072], P(None, ('expert', 'tensor')), may hold values from -0.109375 to 0.109375
- down_weight: bfloat16 [131072, 3072], P(('expert', 'tensor')), may hold values from -0.0625 to 0.0625
- expert_ids: int32 [2048, 4], P(('expert', 'tensor')), may hold values from 0 to 15, all different within a row; in each aligned block of 4 rows (0 to 3, 4 to 7, ...) at most 2 rows name the same one
Outputs:
- hidden_state: bfloat16 [2048, 3072], P(('expert', 'tensor'))
- expert_mix: bfloat16 [2048, 3072], P(('expert', 'tensor'))
The draws below stay inside these ranges and needn't reach their ends.
Inputs may be any that keep to these rules, and one draw needn't show every extreme that they name: `expert_ids`: each row names 4 different experts; among the 4 rows of one device no expert is named more than 2 times.
All inputs are finite; a program needn't handle non-finite values.
Results may differ from the reference program's by a relative error of at most 0.013.
Values may be sent and summed in bfloat16 or wider, within the bound.
No kernel may reach another device: no remote copies, remote signals or barrier semaphores. Data moves between devices by JAX's collectives and lax.ppermute only.
A program may use at most 128 MiB of HBM per device.

```python
import math
import jax
import jax.numpy as jnp
import numpy as np
from jax import lax

D = 3072
HEADS = 24
HD = 128
EXPERTS = 16
TOPK = 4
FF = 8192
TOK_DEV = 4
CAP = 2
TOKENS = 2048
N_EXPERT = 64
N_TENSOR = 8


def block_levels(stream_key, dims, split, least, largest):
    level, own = 1.0, jax.random.fold_in(stream_key, 6)
    for position, shards_of in split:
        heights = jnp.exp(jax.random.uniform(jax.random.fold_in(own, position), (shards_of,), jnp.float32, least / len(split), largest / len(split)))
        level = level * jnp.repeat(heights, dims[position] // shards_of).reshape([-1 if axis == position else 1 for axis in range(len(dims))])
    return level


def routed_block(own_key, own, number, rows, number_of, top, limit, lean):
    order = jax.random.permutation(own_key, number_of)
    crowded, common = portions_of(number_of, rows * top, limit, lean, True), portions_of(number_of, rows * top, limit, lean, False)
    places = jnp.arange(number_of)

    def named(tallies, rotation):
        used = int((tallies > 0).sum())
        fixed = max(1, used // 4)
        shifted = fixed + (places - fixed + rotation * (used - fixed)) % max(1, number_of - fixed)
        return jnp.zeros((number_of,), jnp.int32).at[order[jnp.where(places < fixed, places, shifted)]].set(jnp.asarray(tallies, jnp.int32))

    tallies = jnp.where(number % 4 == 0, named(crowded, number // 4), named(common, number - number // 4 - 1))
    mixed = jax.random.permutation(jax.random.fold_in(own, 3), number_of)
    giver, taker = mixed[0:number_of // 2 * 2:2], mixed[1:number_of // 2 * 2:2]
    slack = jnp.minimum(tallies[giver] - 1, limit - tallies[taker]) // 2
    slack = jnp.where((giver == order[0]) | (taker == order[0]) | (tallies[taker] == 0), 0, jnp.maximum(slack, 0))
    shifted = jax.random.randint(jax.random.fold_in(own, 4), (number_of // 2,), 0, 1 << 20) % (slack + 1)
    tallies = tallies.at[giver].add(-shifted).at[taker].add(shifted)
    labels = jnp.searchsorted(jnp.cumsum(tallies), jnp.arange(rows * top), side="right").astype(jnp.int32)
    listing = labels.reshape(top, rows).T
    listing = listing[jax.random.permutation(jax.random.fold_in(own, 1), rows)]
    rotation = jax.random.randint(jax.random.fold_in(own, 2), (rows, 1), 0, top)
    return jnp.take_along_axis(listing, (jnp.arange(top)[None, :] + rotation) % top, axis=1)


def portions_of(number_of, total, limit, lean, full):
    loads = [(1 << 20) // math.isqrt(standing ** lean) + 1 for standing in range(1, number_of + 1)]
    largest = limit if full else min(limit, max(-(-total // number_of), total * loads[0] // sum(loads)))
    least = 1 if total - largest >= number_of - 1 else 0
    given, rest = [largest] + [least] * (number_of - 1), total - largest - least * (number_of - 1)
    while rest > 0:
        movable = [i for i in range(1, number_of) if given[i] < largest] or [i for i in range(1, number_of) if given[i] < limit]
        mass, budget = sum([loads[i] for i in movable]), rest
        for i in movable:
            extra = min(limit - given[i], max(1, budget * loads[i] // mass), rest)
            given[i] = given[i] + extra
            rest = rest - extra
    return np.array(given)


def scatter_about(key, shape, deviation, limit, pieces=(), held_as=jnp.bfloat16):
    values = jax.random.normal(key, shape, jnp.float32) * deviation
    if len(pieces) > 0:
        values = block_levels(key, shape, pieces, -0.22, 0.18) * values
    return jnp.clip(values, min=-limit, max=limit).astype(held_as)


def setup_inputs(seed: int = 0) -> dict:
    seeds = jax.random.split(jax.random.key(seed), 10)
    context = scatter_about(seeds[0], (TOKENS, HEADS * HD), 1.0, 6.0, ((0, 64), (1, 8)))
    out_weight = scatter_about(seeds[1], (HEADS * HD, D), (HEADS * HD) ** -0.5, 0.109375, ((0, 8), (1, 64)))
    residual = scatter_about(seeds[2], (TOKENS, D), 1.0, 6.0, ((0, 512),))
    norm_gain = jnp.clip(1.0 + 0.18 * jax.random.normal(seeds[3], (D,), jnp.float32), 0.099609375, 1.8984375).astype(jnp.bfloat16)
    router_weight = scatter_about(seeds[4], (D, EXPERTS), D ** -0.5, 0.109375)
    gate_weight = scatter_about(seeds[5], (D, EXPERTS * FF), D ** -0.5, 0.109375, ((1, 512),))
    up_weight = scatter_about(seeds[6], (D, EXPERTS * FF), D ** -0.5, 0.109375, ((1, 512),))
    down_weight = scatter_about(seeds[7], (EXPERTS * FF, D), FF ** -0.5, 0.0625, ((0, 512),))
    expert_ids_keys = jax.random.split(jax.random.fold_in(seeds[8], 1), TOKENS // TOK_DEV)
    expert_ids_turns = jax.random.permutation(jax.random.fold_in(seeds[8], 3), TOKENS // TOK_DEV)
    expert_ids = jax.vmap(lambda own, number: routed_block(jax.random.fold_in(seeds[8], 2), own, number, TOK_DEV, EXPERTS, TOPK, CAP, 1))(expert_ids_keys, expert_ids_turns).reshape((TOKENS, TOPK))
    return dict(context=context, out_weight=out_weight, residual=residual, norm_gain=norm_gain, router_weight=router_weight, gate_weight=gate_weight, up_weight=up_weight, down_weight=down_weight, expert_ids=expert_ids)


norm_epsilon = 1e-05

def layer_norm(state, norm_gain):
    values = state.astype(jnp.float32)
    row_mean = lax.optimization_barrier(jnp.mean(values, axis=-1, keepdims=True))
    centred = values - row_mean
    variance = lax.optimization_barrier(jnp.mean(centred * centred, axis=-1, keepdims=True))
    return (centred * lax.rsqrt(variance + norm_epsilon) * norm_gain.astype(jnp.float32)).astype(jnp.bfloat16)

def reference(context, out_weight, residual, norm_gain, router_weight, gate_weight, up_weight, down_weight, expert_ids):
    attention_sum = jnp.dot(context, out_weight, preferred_element_type=jnp.float32)
    hidden_state = (residual.astype(jnp.float32) + attention_sum).astype(jnp.bfloat16)
    normed = layer_norm(hidden_state, norm_gain)
    logits = jnp.dot(normed, router_weight, preferred_element_type=jnp.float32)
    picked = jnp.take_along_axis(logits, expert_ids, axis=1)
    scores = jnp.exp(picked)
    route_weight = scores / lax.optimization_barrier(jnp.sum(scores, axis=1, keepdims=True))
    devices = N_EXPERT * N_TENSOR
    owner_device = jnp.arange(TOKENS, dtype=jnp.int32) // TOK_DEV
    onehot = (expert_ids[:, :, None] == jnp.arange(EXPERTS, dtype=jnp.int32)[None, None, :]).astype(jnp.int32)
    present = lax.optimization_barrier(jnp.sum(onehot, axis=1)).reshape(devices, TOK_DEV, EXPERTS)
    before = (jnp.cumsum(present, axis=1) - present).reshape(TOKENS, EXPERTS)
    slot_rank = lax.optimization_barrier(jnp.sum(onehot * before[:, None, :], axis=2)).astype(jnp.int32)
    slot_place = (owner_device[:, None] * CAP + slot_rank).astype(jnp.int32)
    slot_total = devices * CAP
    token_index = jnp.broadcast_to(jnp.arange(TOKENS, dtype=jnp.int32)[:, None], (TOKENS, TOPK))
    slot_table = jnp.full((EXPERTS, slot_total), TOKENS, jnp.int32).at[expert_ids, slot_place].set(token_index)
    padded = jnp.concatenate([normed, jnp.zeros((1, D), jnp.bfloat16)], axis=0)
    shares = devices // EXPERTS
    share_width = FF // shares

    def one_expert(expert_index):
        slot_rows = padded[slot_table[expert_index]]
        gate_cols = lax.dynamic_slice_in_dim(gate_weight, expert_index * FF, FF, 1)
        up_cols = lax.dynamic_slice_in_dim(up_weight, expert_index * FF, FF, 1)
        gate_value = jnp.dot(slot_rows, gate_cols, preferred_element_type=jnp.float32)
        up_value = jnp.dot(slot_rows, up_cols, preferred_element_type=jnp.float32)
        hidden = (jax.nn.silu(gate_value) * up_value).astype(jnp.bfloat16)
        down_rows = lax.dynamic_slice_in_dim(down_weight, expert_index * FF, FF, 0)

        def add_share(running, share_index):
            share_piece = lax.dynamic_slice_in_dim(hidden, share_index * share_width, share_width, 1)
            share_down = lax.dynamic_slice_in_dim(down_rows, share_index * share_width, share_width, 0)
            rounded = jnp.dot(share_piece, share_down, preferred_element_type=jnp.float32).astype(jnp.bfloat16)
            rounded = lax.optimization_barrier(rounded)
            return (running + rounded.astype(jnp.float32), None)
        running, _ = lax.scan(add_share, jnp.zeros((slot_total, D), jnp.float32), jnp.arange(shares, dtype=jnp.int32))
        return running
    outputs = lax.map(one_expert, jnp.arange(EXPERTS, dtype=jnp.int32))
    chosen = outputs[expert_ids, slot_place]
    expert_mix = lax.optimization_barrier(jnp.sum(route_weight[:, :, None] * chosen, axis=1)).astype(jnp.bfloat16)
    return (hidden_state, expert_mix)
```

```python
import jax
import jax.numpy as jnp
import numpy as np
from jax import lax
from jax.sharding import Mesh, PartitionSpec as P

CAP = 2
AXES = ("X", "B", "I", "Y", "C")
SIZES = (4, 4, 4, 4, 2)
EXPERT = ("X", "B", "I")
TENSOR = ("Y", "C")

norm_epsilon = 1e-05


def layer_norm(state, norm_gain):
    values = state.astype(jnp.float32)
    row_mean = jnp.mean(values, axis=-1, keepdims=True)
    centred = values - row_mean
    variance = jnp.mean(centred * centred, axis=-1, keepdims=True)
    return (centred * lax.rsqrt(variance + norm_epsilon) * norm_gain.astype(jnp.float32)).astype(
        jnp.bfloat16
    )


def swap(value, axes):
    return lax.all_to_all(value, axes, split_axis=0, concat_axis=0, tiled=True)


def attention_rows(context, out_weight):
    tokens = lax.all_gather(context, "X", axis=0, tiled=True)
    columns = lax.all_gather(out_weight.T, ("B", "I"), axis=0, tiled=True)
    partial_sum = lax.dot_general(
        tokens, columns, (((1,), (1,)), ((), ())), preferred_element_type=jnp.float32
    ).astype(jnp.bfloat16)
    width = columns.shape[0]
    pieces = swap(partial_sum.reshape(32, -1, width), ("X", "Y", "C"))
    pieces = pieces.reshape(4, 8, -1, width).astype(jnp.float32)
    return jnp.transpose(jnp.sum(pieces, axis=1), (1, 0, 2)).reshape(-1, 4 * width)


def both_cores(rows, weights, partner):
    total = None
    for gate, up, down in (weights, partner):
        gate_value = jnp.dot(rows, gate, preferred_element_type=jnp.float32)
        up_value = jnp.dot(rows, up, preferred_element_type=jnp.float32)
        hidden = (jax.nn.silu(gate_value) * up_value).astype(jnp.bfloat16)
        part = jnp.dot(hidden, down, preferred_element_type=jnp.float32)
        total = part if total is None else total + part
    return total.astype(jnp.bfloat16)


def on_device(
    context,
    out_weight,
    residual,
    norm_gain,
    router_weight,
    gate_weight,
    up_weight,
    down_weight,
    expert_ids,
):
    width = residual.shape[1]
    experts = router_weight.shape[1]
    weights = (gate_weight, up_weight, down_weight)
    partner = tuple(lax.ppermute(w, "C", [(0, 1), (1, 0)]) for w in weights)
    attention_sum = attention_rows(context, out_weight)
    hidden_state = (residual.astype(jnp.float32) + attention_sum).astype(jnp.bfloat16)
    normed = layer_norm(hidden_state, norm_gain)
    logits = jnp.dot(normed, router_weight, preferred_element_type=jnp.float32)
    matches = expert_ids[:, :, None] == jnp.arange(experts, dtype=jnp.int32)[None, None, :]
    picked = jnp.sum(jnp.where(matches, logits[:, None, :], 0.0), axis=2)
    scores = jnp.exp(picked)
    route_weight = scores / jnp.sum(scores, axis=1, keepdims=True)
    onehot = matches.astype(jnp.int32)
    present = jnp.sum(onehot, axis=1)
    before = jnp.cumsum(present, axis=0) - present
    slot_rank = jnp.sum(onehot * before[:, None, :], axis=2)
    cell_index = expert_ids * CAP + slot_rank
    cells = cell_index[:, :, None] == jnp.arange(experts * CAP, dtype=jnp.int32)[None, None, :]
    assign = jnp.any(cells, axis=1)
    send_rows = jnp.dot(
        assign.astype(jnp.bfloat16).T, normed, preferred_element_type=jnp.float32
    ).astype(jnp.bfloat16)

    at_x = swap(send_rows.reshape(4, 4 * CAP, width), "X")
    by_z = jnp.transpose(at_x.reshape(4, 4, CAP, width), (1, 0, 2, 3)).reshape(16, CAP, width)
    at_z = swap(by_z, ("B", "I")).reshape(16 * CAP, width)
    block_rows = lax.all_gather(at_z, "I", axis=0, tiled=True)
    rows = lax.all_gather(block_rows, "Y", axis=0, tiled=True)

    partial_value = both_cores(rows, weights, partner)

    def summed(value, axes, parts):
        got = swap(value.reshape(parts, -1, width), axes)
        return jnp.sum(got.astype(jnp.float32), axis=0).astype(jnp.bfloat16)

    over_y = summed(partial_value, "Y", 4)
    over_block = summed(over_y, "I", 4)
    back_z = swap(over_block.reshape(16, CAP, width), ("B", "I"))
    back_x = jnp.transpose(back_z.reshape(4, 4, CAP, width), (1, 0, 2, 3)).reshape(4, 4 * CAP, width)
    chosen = swap(back_x, "X").reshape(experts * CAP, width)
    cell_weight = jnp.sum(jnp.where(cells, route_weight[:, :, None], 0.0), axis=1)
    expert_mix = jnp.dot(
        cell_weight, chosen.astype(jnp.float32), precision=lax.Precision.HIGHEST
    ).astype(jnp.bfloat16)
    return (hidden_state, expert_mix)


def solution(mesh):
    fine = Mesh(np.asarray(mesh.devices).reshape(SIZES), AXES)
    whole = EXPERT + TENSOR
    placed = (
        P(EXPERT, TENSOR),
        P(TENSOR, EXPERT),
        P(whole, None),
        P(),
        P(),
        P(None, whole),
        P(None, whole),
        P(whole, None),
        P(whole, None),
    )
    return jax.shard_map(
        on_device,
        mesh=fine,
        in_specs=placed,
        out_specs=(P(whole, None), P(whole, None)),
        check_vma=False,
    )
```

```python
import jax
import jax.numpy as jnp
import numpy as np
from jax import lax
from jax.experimental import pallas as pl
from jax.experimental.pallas import tpu as pltpu
from jax.sharding import Mesh, PartitionSpec as P

CAP = 2
AXES = ("X", "B", "I", "Y", "C")
SIZES = (4, 4, 4, 4, 2)
EXPERT = ("X", "B", "I")
TENSOR = ("Y", "C")

norm_epsilon = 1e-05


def layer_norm(state, norm_gain):
    values = state.astype(jnp.float32)
    row_mean = jnp.mean(values, axis=-1, keepdims=True)
    centred = values - row_mean
    variance = jnp.mean(centred * centred, axis=-1, keepdims=True)
    return (centred * lax.rsqrt(variance + norm_epsilon) * norm_gain.astype(jnp.float32)).astype(
        jnp.bfloat16
    )


def swap(value, axes):
    return lax.all_to_all(value, axes, split_axis=0, concat_axis=0, tiled=True)


def attention_rows(context, out_weight):
    tokens = lax.all_gather(context, "X", axis=0, tiled=True)
    columns = lax.all_gather(out_weight.T, ("B", "I"), axis=0, tiled=True)
    partial_sum = lax.dot_general(
        tokens, columns, (((1,), (1,)), ((), ())), preferred_element_type=jnp.float32
    ).astype(jnp.bfloat16)
    width = columns.shape[0]
    pieces = swap(partial_sum.reshape(32, -1, width), ("X", "Y", "C"))
    pieces = pieces.reshape(4, 8, -1, width).astype(jnp.float32)
    return jnp.transpose(jnp.sum(pieces, axis=1), (1, 0, 2)).reshape(-1, 4 * width)


def expert_kernel(rows_ref, g0, u0, d0, g1, u1, d1, out_ref, sums):
    depth = rows_ref.shape[1]
    step = 768

    def inner(k, carry):
        at = pl.ds(pl.multiple_of(k * step, step), step)
        piece = rows_ref[:, at]
        for i, weight in enumerate((g0, u0, g1, u1)):
            sums[i] += jnp.dot(piece, weight[at, :], preferred_element_type=jnp.float32)
        return carry

    sums[...] = jnp.zeros_like(sums)
    lax.fori_loop(0, depth // step, inner, 0)
    first = (jax.nn.silu(sums[0]) * sums[1]).astype(jnp.bfloat16)
    second = (jax.nn.silu(sums[2]) * sums[3]).astype(jnp.bfloat16)

    def outer(k, carry):
        at = pl.ds(pl.multiple_of(k * step, step), step)
        total = jnp.dot(first, d0[:, at], preferred_element_type=jnp.float32)
        total += jnp.dot(second, d1[:, at], preferred_element_type=jnp.float32)
        out_ref[:, at] = total.astype(jnp.bfloat16)
        return carry

    lax.fori_loop(0, depth // step, outer, 0)


def both_cores(rows, weights, partner):
    count, width = rows.shape
    units = weights[0].shape[1]
    vmem = pl.BlockSpec(memory_space=pltpu.VMEM)
    return pl.pallas_call(
        expert_kernel,
        out_shape=jax.ShapeDtypeStruct((count, width), jnp.bfloat16),
        in_specs=[vmem] * 7,
        out_specs=vmem,
        scratch_shapes=[pltpu.VMEM((4, count, units), jnp.float32)],
        compiler_params=pltpu.CompilerParams(vmem_limit_bytes=32 * 1024 * 1024),
        cost_estimate=pl.CostEstimate(
            flops=12 * count * width * units,
            bytes_accessed=4 * count * width + 12 * width * units,
            transcendentals=2 * count * units,
        ),
    )(rows, *weights, *partner)


def on_device(
    context,
    out_weight,
    residual,
    norm_gain,
    router_weight,
    gate_weight,
    up_weight,
    down_weight,
    expert_ids,
):
    width = residual.shape[1]
    experts = router_weight.shape[1]
    weights = (gate_weight, up_weight, down_weight)
    partner = tuple(lax.ppermute(w, "C", [(0, 1), (1, 0)]) for w in weights)
    attention_sum = attention_rows(context, out_weight)
    hidden_state = (residual.astype(jnp.float32) + attention_sum).astype(jnp.bfloat16)
    normed = layer_norm(hidden_state, norm_gain)
    logits = jnp.dot(normed, router_weight, preferred_element_type=jnp.float32)
    matches = expert_ids[:, :, None] == jnp.arange(experts, dtype=jnp.int32)[None, None, :]
    picked = jnp.sum(jnp.where(matches, logits[:, None, :], 0.0), axis=2)
    scores = jnp.exp(picked)
    route_weight = scores / jnp.sum(scores, axis=1, keepdims=True)
    onehot = matches.astype(jnp.int32)
    present = jnp.sum(onehot, axis=1)
    before = jnp.cumsum(present, axis=0) - present
    slot_rank = jnp.sum(onehot * before[:, None, :], axis=2)
    cell_index = expert_ids * CAP + slot_rank
    cells = cell_index[:, :, None] == jnp.arange(experts * CAP, dtype=jnp.int32)[None, None, :]
    assign = jnp.any(cells, axis=1)
    send_rows = jnp.dot(
        assign.astype(jnp.bfloat16).T, normed, preferred_element_type=jnp.float32
    ).astype(jnp.bfloat16)

    at_x = swap(send_rows.reshape(4, 4 * CAP, width), "X")
    by_z = jnp.transpose(at_x.reshape(4, 4, CAP, width), (1, 0, 2, 3)).reshape(16, CAP, width)
    at_z = swap(by_z, ("B", "I")).reshape(16 * CAP, width)
    block_rows = lax.all_gather(at_z, "I", axis=0, tiled=True)

    def turn(value, by):
        return lax.ppermute(value, "Y", [(i, (i + by) % 4) for i in range(4)])

    half = block_rows.shape[0] // 2
    below, above = turn(block_rows, 1), turn(block_rows, -1)
    far = jnp.concatenate([turn(below[:half], 1), turn(above[half:], -1)], axis=0)
    near = both_cores(jnp.concatenate([below, above], axis=0), weights, partner)
    to_below, to_above = turn(near[: 2 * half], -1), turn(near[2 * half :], 1)
    to_far = turn(both_cores(far, weights, partner), 2)
    own = both_cores(block_rows, weights, partner)
    over_y = own.astype(jnp.float32) + to_far.astype(jnp.float32)
    over_y += to_below.astype(jnp.float32) + to_above.astype(jnp.float32)
    over_y = over_y.astype(jnp.bfloat16)

    def summed(value, axes, parts):
        got = swap(value.reshape(parts, -1, width), axes)
        return jnp.sum(got.astype(jnp.float32), axis=0).astype(jnp.bfloat16)

    over_block = summed(over_y, "I", 4)
    back_z = swap(over_block.reshape(16, CAP, width), ("B", "I"))
    back_x = jnp.transpose(back_z.reshape(4, 4, CAP, width), (1, 0, 2, 3)).reshape(4, 4 * CAP, width)
    chosen = swap(back_x, "X").reshape(experts * CAP, width)
    cell_weight = jnp.sum(jnp.where(cells, route_weight[:, :, None], 0.0), axis=1)
    expert_mix = jnp.dot(
        cell_weight, chosen.astype(jnp.float32), precision=lax.Precision.HIGHEST
    ).astype(jnp.bfloat16)
    return (hidden_state, expert_mix)


def solution(mesh):
    fine = Mesh(np.asarray(mesh.devices).reshape(SIZES), AXES)
    whole = EXPERT + TENSOR
    placed = (
        P(EXPERT, TENSOR),
        P(TENSOR, EXPERT),
        P(whole, None),
        P(),
        P(),
        P(None, whole),
        P(None, whole),
        P(whole, None),
        P(whole, None),
    )
    return jax.shard_map(
        on_device,
        mesh=fine,
        in_specs=placed,
        out_specs=(P(whole, None), P(whole, None)),
        check_vma=False,
    )
```

```python
import functools

import jax
import jax.numpy as jnp
import numpy as np
from jax import lax
from jax.experimental import pallas as pl
from jax.experimental.pallas import tpu as pltpu
from jax.sharding import Mesh, PartitionSpec as P

CAP = 2
AXES = ("X", "B", "I", "Y", "C")
SIZES = (4, 4, 4, 4, 2)
EXPERT = ("X", "B", "I")
TENSOR = ("Y", "C")

norm_epsilon = 1e-05


def layer_norm(state, norm_gain):
    values = state.astype(jnp.float32)
    row_mean = jnp.mean(values, axis=-1, keepdims=True)
    centred = values - row_mean
    variance = jnp.mean(centred * centred, axis=-1, keepdims=True)
    return (centred * lax.rsqrt(variance + norm_epsilon) * norm_gain.astype(jnp.float32)).astype(
        jnp.bfloat16
    )


def swap(value, axes):
    return lax.all_to_all(value, axes, split_axis=0, concat_axis=0, tiled=True)


def spread(value, axes, parts):
    return swap(jnp.broadcast_to(value[None], (parts,) + value.shape), axes)


def attention_rows(context, out_weight):
    tokens = spread(context, ("X", "I"), 16).reshape(-1, context.shape[1])
    columns = spread(out_weight.T, "B", 4).reshape(-1, out_weight.shape[0])
    partial_sum = lax.dot_general(
        tokens, columns, (((1,), (1,)), ((), ())), preferred_element_type=jnp.float32
    ).astype(jnp.bfloat16)
    width = columns.shape[0]
    pieces = swap(partial_sum.reshape(128, -1, width), ("X", "I", "Y", "C"))
    count = pieces.shape[1]
    pieces = pieces.reshape(16, 8, count, width).astype(jnp.float32)
    summed = jnp.sum(pieces, axis=1).reshape(4, 4, count, 4, width // 4)
    return jnp.transpose(summed, (2, 0, 3, 1, 4)).reshape(count, 16 * width)


def expert_kernel(layout, *refs):
    pieces = sum(len(group) for group in layout)
    inputs, refs = refs[:pieces], refs[pieces:]
    g0, u0, d0, g1, u1, d1 = refs[:6]
    results, sums = refs[6 : 6 + len(layout)], refs[-1]
    step = results[0].shape[2]
    rows = results[0].shape[1]
    sums[...] = jnp.zeros_like(sums)
    for part in range(results[0].shape[0]):
        at = slice(part * step, (part + 1) * step)
        held = []
        first = 0
        for group in layout:
            left = part
            for number, parts in enumerate(group):
                if 0 <= left < parts:
                    held.append(inputs[first + number][left])
                left -= parts
            first += len(group)
        piece = jnp.concatenate(held, axis=0) if len(held) > 1 else held[0]
        for i, weight in enumerate((g0, u0, g1, u1)):
            sums[i] += jnp.dot(piece, weight[at, :], preferred_element_type=jnp.float32)
    first = (jax.nn.silu(sums[0]) * sums[1]).astype(jnp.bfloat16)
    second = (jax.nn.silu(sums[2]) * sums[3]).astype(jnp.bfloat16)
    for part in range(results[0].shape[0]):
        at = slice(part * step, (part + 1) * step)
        total = jnp.dot(first, d0[:, at], preferred_element_type=jnp.float32)
        total += jnp.dot(second, d1[:, at], preferred_element_type=jnp.float32)
        total = total.astype(jnp.bfloat16)
        for number, result in enumerate(results):
            result[part] = total[number * rows : (number + 1) * rows]


def both_cores(groups, weights, partner):
    layout = tuple(tuple(p.shape[0] for p in group) for group in groups)
    parts, (rows, step) = sum(layout[0]), groups[0][0].shape[1:]
    count, width, units = rows * len(groups), parts * step, weights[0].shape[1]
    vmem = pl.BlockSpec(memory_space=pltpu.VMEM)
    flat = [p for group in groups for p in group]
    return pl.pallas_call(
        functools.partial(expert_kernel, layout),
        out_shape=[jax.ShapeDtypeStruct((parts, rows, step), jnp.bfloat16)] * len(groups),
        in_specs=[vmem] * (len(flat) + 6),
        out_specs=[vmem] * len(groups),
        scratch_shapes=[pltpu.VMEM((4, count, units), jnp.float32)],
        compiler_params=pltpu.CompilerParams(vmem_limit_bytes=32 * 1024 * 1024),
        cost_estimate=pl.CostEstimate(
            flops=12 * count * width * units,
            bytes_accessed=4 * count * width + 12 * width * units,
            transcendentals=2 * count * units,
        ),
    )(*flat, *weights, *partner)


def on_device(
    context,
    out_weight,
    residual,
    norm_gain,
    router_weight,
    gate_weight,
    up_weight,
    down_weight,
    expert_ids,
):
    width = residual.shape[1]
    experts = router_weight.shape[1]
    weights = (gate_weight, up_weight, down_weight)
    partner = tuple(lax.ppermute(w, "C", [(0, 1), (1, 0)]) for w in weights)
    attention_sum = attention_rows(context, out_weight)
    hidden_state = (residual.astype(jnp.float32) + attention_sum).astype(jnp.bfloat16)
    normed = layer_norm(hidden_state, norm_gain)
    logits = jnp.dot(normed, router_weight, preferred_element_type=jnp.float32)
    matches = expert_ids[:, :, None] == jnp.arange(experts, dtype=jnp.int32)[None, None, :]
    picked = jnp.sum(jnp.where(matches, logits[:, None, :], 0.0), axis=2)
    scores = jnp.exp(picked)
    route_weight = scores / jnp.sum(scores, axis=1, keepdims=True)
    onehot = matches.astype(jnp.int32)
    present = jnp.sum(onehot, axis=1)
    before = jnp.cumsum(present, axis=0) - present
    slot_rank = jnp.sum(onehot * before[:, None, :], axis=2)
    cell_index = expert_ids * CAP + slot_rank
    cells = cell_index[:, :, None] == jnp.arange(experts * CAP, dtype=jnp.int32)[None, None, :]
    assign = jnp.any(cells, axis=1)
    send_rows = jnp.dot(
        assign.astype(jnp.bfloat16).T, normed, preferred_element_type=jnp.float32
    ).astype(jnp.bfloat16)

    quarter = width // 4
    outgoing = jnp.transpose(send_rows.reshape(experts, CAP, 4, quarter), (0, 2, 1, 3))
    landed = swap(outgoing.reshape(4 * experts, CAP, quarter), EXPERT)
    block_rows = spread(landed.reshape(-1, quarter), "I", 4)

    def turn(value, by):
        return lax.ppermute(value, "Y", [(i, (i + by) % 4) for i in range(4)])

    below, above = turn(block_rows, 1), turn(block_rows, -1)
    far = [turn(below[:2], 1), turn(above[2:], -1)]
    near_below, near_above = both_cores([[below], [above]], weights, partner)
    to_below, to_above = turn(near_below, -1), turn(near_above, 1)
    to_far = turn(both_cores([far], weights, partner)[0], 2)
    own = both_cores([[block_rows]], weights, partner)[0]
    over_y = own.astype(jnp.float32) + to_far.astype(jnp.float32)
    over_y += to_below.astype(jnp.float32) + to_above.astype(jnp.float32)
    over_y = over_y.astype(jnp.bfloat16)

    over_block = jnp.sum(swap(over_y, "I").astype(jnp.float32), axis=0).astype(jnp.bfloat16)
    back = swap(over_block.reshape(4 * experts, CAP, quarter), EXPERT)
    chosen = jnp.transpose(back.reshape(experts, 4, CAP, quarter), (0, 2, 1, 3))
    chosen = chosen.reshape(experts * CAP, width)
    cell_weight = jnp.sum(jnp.where(cells, route_weight[:, :, None], 0.0), axis=1)
    expert_mix = jnp.dot(
        cell_weight, chosen.astype(jnp.float32), precision=lax.Precision.HIGHEST
    ).astype(jnp.bfloat16)
    return (hidden_state, expert_mix)


def solution(mesh):
    fine = Mesh(np.asarray(mesh.devices).reshape(SIZES), AXES)
    whole = EXPERT + TENSOR
    placed = (
        P(EXPERT, TENSOR),
        P(TENSOR, EXPERT),
        P(whole, None),
        P(),
        P(),
        P(None, whole),
        P(None, whole),
        P(whole, None),
        P(whole, None),
    )
    return jax.shard_map(
        on_device,
        mesh=fine,
        in_specs=placed,
        out_specs=(P(whole, None), P(whole, None)),
        check_vma=False,
    )
```

```python
import functools

import jax
import jax.numpy as jnp
import numpy as np
from jax import lax
from jax.experimental import pallas as pl
from jax.experimental.pallas import tpu as pltpu
from jax.sharding import Mesh, PartitionSpec as P

CAP = 2
AXES = ("X", "B", "I", "Y", "C")
SIZES = (4, 4, 4, 4, 2)
EXPERT = ("X", "B", "I")
TENSOR = ("Y", "C")

norm_epsilon = 1e-05


def layer_norm(state, norm_gain):
    values = state.astype(jnp.float32)
    row_mean = jnp.mean(values, axis=-1, keepdims=True)
    centred = values - row_mean
    variance = jnp.mean(centred * centred, axis=-1, keepdims=True)
    return (centred * lax.rsqrt(variance + norm_epsilon) * norm_gain.astype(jnp.float32)).astype(
        jnp.bfloat16
    )


def swap(value, axes):
    return lax.all_to_all(value, axes, split_axis=0, concat_axis=0, tiled=True)


def attention_rows(context, out_weight):
    tokens = lax.all_gather(context, "X", axis=0, tiled=True)
    columns = lax.all_gather(out_weight.T, ("B", "I"), axis=0, tiled=True)
    partial_sum = lax.dot_general(
        tokens, columns, (((1,), (1,)), ((), ())), preferred_element_type=jnp.float32
    ).astype(jnp.bfloat16)
    width = columns.shape[0]
    pieces = swap(partial_sum.reshape(32, -1, width), ("X", "Y", "C"))
    pieces = pieces.reshape(4, 8, -1, width).astype(jnp.float32)
    return jnp.transpose(jnp.sum(pieces, axis=1), (1, 0, 2)).reshape(-1, 4 * width)


def expert_kernel(layout, *refs):
    pieces = sum(len(group) for group in layout)
    inputs, refs = refs[:pieces], refs[pieces:]
    g0, u0, d0, g1, u1, d1 = refs[:6]
    results, sums = refs[6 : 6 + len(layout)], refs[-1]
    step = results[0].shape[2]
    rows = results[0].shape[1]
    sums[...] = jnp.zeros_like(sums)
    for part in range(results[0].shape[0]):
        at = slice(part * step, (part + 1) * step)
        held = []
        first = 0
        for group in layout:
            left = part
            for number, parts in enumerate(group):
                if 0 <= left < parts:
                    held.append(inputs[first + number][left])
                left -= parts
            first += len(group)
        piece = jnp.concatenate(held, axis=0) if len(held) > 1 else held[0]
        for i, weight in enumerate((g0, u0, g1, u1)):
            sums[i] += jnp.dot(piece, weight[at, :], preferred_element_type=jnp.float32)
    first = (jax.nn.silu(sums[0]) * sums[1]).astype(jnp.bfloat16)
    second = (jax.nn.silu(sums[2]) * sums[3]).astype(jnp.bfloat16)
    for part in range(results[0].shape[0]):
        at = slice(part * step, (part + 1) * step)
        total = jnp.dot(first, d0[:, at], preferred_element_type=jnp.float32)
        total += jnp.dot(second, d1[:, at], preferred_element_type=jnp.float32)
        total = total.astype(jnp.bfloat16)
        for number, result in enumerate(results):
            result[part] = total[number * rows : (number + 1) * rows]


def both_cores(groups, weights, partner):
    layout = tuple(tuple(p.shape[0] for p in group) for group in groups)
    parts, (rows, step) = sum(layout[0]), groups[0][0].shape[1:]
    count, width, units = rows * len(groups), parts * step, weights[0].shape[1]
    vmem = pl.BlockSpec(memory_space=pltpu.VMEM)
    flat = [p for group in groups for p in group]
    return pl.pallas_call(
        functools.partial(expert_kernel, layout),
        out_shape=[jax.ShapeDtypeStruct((parts, rows, step), jnp.bfloat16)] * len(groups),
        in_specs=[vmem] * (len(flat) + 6),
        out_specs=[vmem] * len(groups),
        scratch_shapes=[pltpu.VMEM((4, count, units), jnp.float32)],
        compiler_params=pltpu.CompilerParams(vmem_limit_bytes=32 * 1024 * 1024),
        cost_estimate=pl.CostEstimate(
            flops=12 * count * width * units,
            bytes_accessed=4 * count * width + 12 * width * units,
            transcendentals=2 * count * units,
        ),
    )(*flat, *weights, *partner)


def on_device(
    context,
    out_weight,
    residual,
    norm_gain,
    router_weight,
    gate_weight,
    up_weight,
    down_weight,
    expert_ids,
):
    width = residual.shape[1]
    experts = router_weight.shape[1]
    weights = (gate_weight, up_weight, down_weight)
    partner = tuple(lax.ppermute(w, "C", [(0, 1), (1, 0)]) for w in weights)
    attention_sum = attention_rows(context, out_weight)
    hidden_state = (residual.astype(jnp.float32) + attention_sum).astype(jnp.bfloat16)
    normed = layer_norm(hidden_state, norm_gain)
    logits = jnp.dot(normed, router_weight, preferred_element_type=jnp.float32)
    matches = expert_ids[:, :, None] == jnp.arange(experts, dtype=jnp.int32)[None, None, :]
    picked = jnp.sum(jnp.where(matches, logits[:, None, :], 0.0), axis=2)
    scores = jnp.exp(picked)
    route_weight = scores / jnp.sum(scores, axis=1, keepdims=True)
    onehot = matches.astype(jnp.int32)
    present = jnp.sum(onehot, axis=1)
    before = jnp.cumsum(present, axis=0) - present
    slot_rank = jnp.sum(onehot * before[:, None, :], axis=2)
    cell_index = expert_ids * CAP + slot_rank
    cells = cell_index[:, :, None] == jnp.arange(experts * CAP, dtype=jnp.int32)[None, None, :]
    assign = jnp.any(cells, axis=1)
    send_rows = jnp.dot(
        assign.astype(jnp.bfloat16).T, normed, preferred_element_type=jnp.float32
    ).astype(jnp.bfloat16)

    send_rows, partner = lax.optimization_barrier((send_rows, partner))
    quarter = width // 4
    outgoing = jnp.transpose(send_rows.reshape(experts, CAP, 4, quarter), (0, 2, 1, 3))
    landed = swap(outgoing.reshape(4 * experts, CAP, quarter), EXPERT)
    block_rows = lax.all_gather(landed.reshape(-1, quarter), "I")

    def turn(value, by):
        return lax.ppermute(value, "Y", [(i, (i + by) % 4) for i in range(4)])

    below, above = turn(block_rows, 1), turn(block_rows, -1)
    far = [turn(below[:2], 1), turn(above[2:], -1)]
    near_below, near_above = both_cores([[below], [above]], weights, partner)
    to_below, to_above = turn(near_below, -1), turn(near_above, 1)
    to_far = turn(both_cores([far], weights, partner)[0], 2)
    own = both_cores([[block_rows]], weights, partner)[0]
    over_y = own.astype(jnp.float32) + to_far.astype(jnp.float32)
    over_y += to_below.astype(jnp.float32) + to_above.astype(jnp.float32)
    over_y = over_y.astype(jnp.bfloat16)

    over_block = jnp.sum(swap(over_y, "I").astype(jnp.float32), axis=0).astype(jnp.bfloat16)
    back = swap(over_block.reshape(4 * experts, CAP, quarter), EXPERT)
    chosen = jnp.transpose(back.reshape(experts, 4, CAP, quarter), (0, 2, 1, 3))
    chosen = chosen.reshape(experts * CAP, width)
    cell_weight = jnp.sum(jnp.where(cells, route_weight[:, :, None], 0.0), axis=1)
    expert_mix = jnp.dot(
        cell_weight, chosen.astype(jnp.float32), precision=lax.Precision.HIGHEST
    ).astype(jnp.bfloat16)
    return (hidden_state, expert_mix)


def solution(mesh):
    fine = Mesh(np.asarray(mesh.devices).reshape(SIZES), AXES)
    whole = EXPERT + TENSOR
    placed = (
        P(EXPERT, TENSOR),
        P(TENSOR, EXPERT),
        P(whole, None),
        P(),
        P(),
        P(None, whole),
        P(None, whole),
        P(whole, None),
        P(whole, None),
    )
    return jax.shard_map(
        on_device,
        mesh=fine,
        in_specs=placed,
        out_specs=(P(whole, None), P(whole, None)),
        check_vma=False,
    )
```

```python
import functools

import jax
import jax.numpy as jnp
import numpy as np
from jax import lax
from jax.experimental import pallas as pl
from jax.experimental.pallas import tpu as pltpu
from jax.sharding import Mesh, PartitionSpec as P

CAP = 2
AXES = ("X", "B", "I", "Y", "C")
SIZES = (4, 4, 4, 4, 2)
EXPERT = ("X", "B", "I")
TENSOR = ("Y", "C")

norm_epsilon = 1e-05


def layer_norm(state, norm_gain):
    values = state.astype(jnp.float32)
    row_mean = jnp.mean(values, axis=-1, keepdims=True)
    centred = values - row_mean
    variance = jnp.mean(centred * centred, axis=-1, keepdims=True)
    return (centred * lax.rsqrt(variance + norm_epsilon) * norm_gain.astype(jnp.float32)).astype(
        jnp.bfloat16
    )


def swap(value, axes):
    return lax.all_to_all(value, axes, split_axis=0, concat_axis=0, tiled=True)


def spread(value, axes, parts):
    return swap(jnp.broadcast_to(value[None], (parts,) + value.shape), axes)


def attention_rows(context, out_weight, weights):
    tokens = spread(context, "X", 4).reshape(-1, context.shape[1])
    columns = lax.all_gather(out_weight.T, ("B", "I"), axis=0, tiled=True)
    partial_sum = lax.dot_general(
        tokens, columns, (((1,), (1,)), ((), ())), preferred_element_type=jnp.float32
    ).astype(jnp.bfloat16)
    partial_sum, *weights = lax.optimization_barrier((partial_sum, *weights))
    partner = tuple(lax.ppermute(w, "C", [(0, 1), (1, 0)]) for w in weights)
    width = columns.shape[0]
    pieces = swap(partial_sum.reshape(32, -1, width), ("X", "Y", "C"))
    pieces = pieces.reshape(4, 8, -1, width).astype(jnp.float32)
    summed = jnp.transpose(jnp.sum(pieces, axis=1), (1, 0, 2)).reshape(-1, 4 * width)
    return summed, partner


def expert_kernel(layout, *refs):
    pieces = sum(len(group) for group in layout)
    inputs, refs = refs[:pieces], refs[pieces:]
    g0, u0, d0, g1, u1, d1 = refs[:6]
    results, sums = refs[6 : 6 + len(layout)], refs[-1]
    step = results[0].shape[2]
    rows = results[0].shape[1]
    sums[...] = jnp.zeros_like(sums)
    for part in range(results[0].shape[0]):
        at = slice(part * step, (part + 1) * step)
        held = []
        first = 0
        for group in layout:
            left = part
            for number, parts in enumerate(group):
                if 0 <= left < parts:
                    held.append(inputs[first + number][left])
                left -= parts
            first += len(group)
        piece = jnp.concatenate(held, axis=0) if len(held) > 1 else held[0]
        for i, weight in enumerate((g0, u0, g1, u1)):
            sums[i] += jnp.dot(piece, weight[at, :], preferred_element_type=jnp.float32)
    first = (jax.nn.silu(sums[0]) * sums[1]).astype(jnp.bfloat16)
    second = (jax.nn.silu(sums[2]) * sums[3]).astype(jnp.bfloat16)
    for part in range(results[0].shape[0]):
        at = slice(part * step, (part + 1) * step)
        total = jnp.dot(first, d0[:, at], preferred_element_type=jnp.float32)
        total += jnp.dot(second, d1[:, at], preferred_element_type=jnp.float32)
        total = total.astype(jnp.bfloat16)
        for number, result in enumerate(results):
            result[part] = total[number * rows : (number + 1) * rows]


def both_cores(groups, weights, partner):
    layout = tuple(tuple(p.shape[0] for p in group) for group in groups)
    parts, (rows, step) = sum(layout[0]), groups[0][0].shape[1:]
    count, width, units = rows * len(groups), parts * step, weights[0].shape[1]
    vmem = pl.BlockSpec(memory_space=pltpu.VMEM)
    flat = [p for group in groups for p in group]
    return pl.pallas_call(
        functools.partial(expert_kernel, layout),
        out_shape=[jax.ShapeDtypeStruct((parts, rows, step), jnp.bfloat16)] * len(groups),
        in_specs=[vmem] * (len(flat) + 6),
        out_specs=[vmem] * len(groups),
        scratch_shapes=[pltpu.VMEM((4, count, units), jnp.float32)],
        compiler_params=pltpu.CompilerParams(vmem_limit_bytes=32 * 1024 * 1024),
        cost_estimate=pl.CostEstimate(
            flops=12 * count * width * units,
            bytes_accessed=4 * count * width + 12 * width * units,
            transcendentals=2 * count * units,
        ),
    )(*flat, *weights, *partner)


def over_block(value):
    return jnp.sum(swap(value, "I").astype(jnp.float32), axis=0)


def on_device(
    context,
    out_weight,
    residual,
    norm_gain,
    router_weight,
    gate_weight,
    up_weight,
    down_weight,
    expert_ids,
):
    width = residual.shape[1]
    experts = router_weight.shape[1]
    weights = (gate_weight, up_weight, down_weight)
    attention_sum, partner = attention_rows(context, out_weight, weights)
    hidden_state = (residual.astype(jnp.float32) + attention_sum).astype(jnp.bfloat16)
    normed = layer_norm(hidden_state, norm_gain)
    logits = jnp.dot(normed, router_weight, preferred_element_type=jnp.float32)
    matches = expert_ids[:, :, None] == jnp.arange(experts, dtype=jnp.int32)[None, None, :]
    picked = jnp.sum(jnp.where(matches, logits[:, None, :], 0.0), axis=2)
    scores = jnp.exp(picked)
    route_weight = scores / jnp.sum(scores, axis=1, keepdims=True)
    onehot = matches.astype(jnp.int32)
    present = jnp.sum(onehot, axis=1)
    before = jnp.cumsum(present, axis=0) - present
    slot_rank = jnp.sum(onehot * before[:, None, :], axis=2)
    cell_index = expert_ids * CAP + slot_rank
    cells = cell_index[:, :, None] == jnp.arange(experts * CAP, dtype=jnp.int32)[None, None, :]
    assign = jnp.any(cells, axis=1)
    send_rows = jnp.dot(
        assign.astype(jnp.bfloat16).T, normed, preferred_element_type=jnp.float32
    ).astype(jnp.bfloat16)

    quarter = width // 4
    outgoing = jnp.transpose(send_rows.reshape(experts, CAP, 4, quarter), (0, 2, 1, 3))
    landed = swap(outgoing.reshape(4 * experts, CAP, quarter), EXPERT)
    landed, partner = lax.optimization_barrier((landed, partner))
    block_rows = lax.all_gather(landed.reshape(-1, quarter), "I")

    def turn(value, by):
        return lax.ppermute(value, "Y", [(i, (i + by) % 4) for i in range(4)])

    low, high = block_rows[:2], block_rows[2:]
    below_low, above_high = turn(low, 1), turn(high, -1)
    below_high, above_low = turn(high, 1), turn(low, -1)
    far = [turn(below_low, 1), turn(above_high, -1)]
    near_below, near_above = both_cores(
        [[below_low, below_high], [above_low, above_high]], weights, partner
    )
    *far, near_below, near_above = lax.optimization_barrier((*far, near_below, near_above))
    to_below, to_above = turn(near_below, -1), turn(near_above, 1)
    far_block = over_block(both_cores([far], weights, partner)[0])
    to_far = turn(far_block.astype(jnp.bfloat16), 2)
    own = both_cores([[block_rows]], weights, partner)[0]
    near = own.astype(jnp.float32) + to_below.astype(jnp.float32) + to_above.astype(jnp.float32)
    summed = over_block(near.astype(jnp.bfloat16)) + to_far.astype(jnp.float32)
    back = swap(summed.astype(jnp.bfloat16).reshape(4 * experts, CAP, quarter), EXPERT)
    chosen = jnp.transpose(back.reshape(experts, 4, CAP, quarter), (0, 2, 1, 3))
    chosen = chosen.reshape(experts * CAP, width)
    cell_weight = jnp.sum(jnp.where(cells, route_weight[:, :, None], 0.0), axis=1)
    expert_mix = jnp.dot(
        cell_weight, chosen.astype(jnp.float32), precision=lax.Precision.HIGHEST
    ).astype(jnp.bfloat16)
    return (hidden_state, expert_mix)


def solution(mesh):
    fine = Mesh(np.asarray(mesh.devices).reshape(SIZES), AXES)
    whole = EXPERT + TENSOR
    placed = (
        P(EXPERT, TENSOR),
        P(TENSOR, EXPERT),
        P(whole, None),
        P(),
        P(),
        P(None, whole),
        P(None, whole),
        P(whole, None),
        P(whole, None),
    )
    return jax.shard_map(
        on_device,
        mesh=fine,
        in_specs=placed,
        out_specs=(P(whole, None), P(whole, None)),
        check_vma=False,
    )
```

```python
import functools

import jax
import jax.numpy as jnp
import numpy as np
from jax import lax
from jax.experimental import pallas as pl
from jax.experimental.pallas import tpu as pltpu
from jax.sharding import Mesh, PartitionSpec as P

CAP = 2
AXES = ("X", "B", "I", "Y", "C")
SIZES = (4, 4, 4, 4, 2)
EXPERT = ("X", "B", "I")
TENSOR = ("Y", "C")

norm_epsilon = 1e-05


def layer_norm(state, norm_gain):
    values = state.astype(jnp.float32)
    row_mean = jnp.mean(values, axis=-1, keepdims=True)
    centred = values - row_mean
    variance = jnp.mean(centred * centred, axis=-1, keepdims=True)
    return (centred * lax.rsqrt(variance + norm_epsilon) * norm_gain.astype(jnp.float32)).astype(
        jnp.bfloat16
    )


def swap(value, axes):
    return lax.all_to_all(value, axes, split_axis=0, concat_axis=0, tiled=True)


def spread(value, axes, parts):
    return swap(jnp.broadcast_to(value[None], (parts,) + value.shape), axes)


def attention_rows(context, out_weight, weights, later):
    tokens = spread(context, "X", 4).reshape(-1, context.shape[1])
    columns = lax.all_gather(out_weight.T, ("B", "I"), axis=0, tiled=True)
    partial_sum = lax.dot_general(
        tokens, columns, (((1,), (1,)), ((), ())), preferred_element_type=jnp.float32
    ).astype(jnp.bfloat16)
    partial_sum, weights, later = lax.optimization_barrier((partial_sum, weights, later))
    partner = tuple(lax.ppermute(w, "C", [(0, 1), (1, 0)]) for w in weights)
    width = columns.shape[0]
    pieces = swap(partial_sum.reshape(32, -1, width), ("X", "Y", "C"))
    pieces = pieces.reshape(4, 8, -1, width).astype(jnp.float32)
    summed = jnp.transpose(jnp.sum(pieces, axis=1), (1, 0, 2)).reshape(-1, 4 * width)
    return summed, partner, later


def expert_kernel(layout, *refs):
    pieces = sum(len(group) for group in layout)
    inputs, refs = refs[:pieces], refs[pieces:]
    g0, u0, d0, g1, u1, d1 = refs[:6]
    results, sums = refs[6 : 6 + len(layout)], refs[-1]
    step = results[0].shape[2]
    rows = results[0].shape[1]
    sums[...] = jnp.zeros_like(sums)
    for part in range(results[0].shape[0]):
        at = slice(part * step, (part + 1) * step)
        held = []
        first = 0
        for group in layout:
            left = part
            for number, parts in enumerate(group):
                if 0 <= left < parts:
                    held.append(inputs[first + number][left])
                left -= parts
            first += len(group)
        piece = jnp.concatenate(held, axis=0) if len(held) > 1 else held[0]
        for i, weight in enumerate((g0, u0, g1, u1)):
            sums[i] += jnp.dot(piece, weight[at, :], preferred_element_type=jnp.float32)
    first = (jax.nn.silu(sums[0]) * sums[1]).astype(jnp.bfloat16)
    second = (jax.nn.silu(sums[2]) * sums[3]).astype(jnp.bfloat16)
    for part in range(results[0].shape[0]):
        at = slice(part * step, (part + 1) * step)
        total = jnp.dot(first, d0[:, at], preferred_element_type=jnp.float32)
        total += jnp.dot(second, d1[:, at], preferred_element_type=jnp.float32)
        total = total.astype(jnp.bfloat16)
        for number, result in enumerate(results):
            result[part] = total[number * rows : (number + 1) * rows]


def both_cores(groups, weights, partner):
    layout = tuple(tuple(p.shape[0] for p in group) for group in groups)
    parts, (rows, step) = sum(layout[0]), groups[0][0].shape[1:]
    count, width, units = rows * len(groups), parts * step, weights[0].shape[1]
    vmem = pl.BlockSpec(memory_space=pltpu.VMEM)
    flat = [p for group in groups for p in group]
    return pl.pallas_call(
        functools.partial(expert_kernel, layout),
        out_shape=[jax.ShapeDtypeStruct((parts, rows, step), jnp.bfloat16)] * len(groups),
        in_specs=[vmem] * (len(flat) + 6),
        out_specs=[vmem] * len(groups),
        scratch_shapes=[pltpu.VMEM((4, count, units), jnp.float32)],
        compiler_params=pltpu.CompilerParams(vmem_limit_bytes=32 * 1024 * 1024),
        cost_estimate=pl.CostEstimate(
            flops=12 * count * width * units,
            bytes_accessed=4 * count * width + 12 * width * units,
            transcendentals=2 * count * units,
        ),
    )(*flat, *weights, *partner)


def over_block(value):
    return jnp.sum(swap(value, "I").astype(jnp.float32), axis=0)


def on_device(
    context,
    out_weight,
    residual,
    norm_gain,
    router_weight,
    gate_weight,
    up_weight,
    down_weight,
    expert_ids,
):
    width = residual.shape[1]
    experts = router_weight.shape[1]
    weights = (gate_weight, up_weight, down_weight)
    attention_sum, partner, (expert_ids, norm_gain) = attention_rows(
        context, out_weight, weights, (expert_ids, norm_gain)
    )
    hidden_state = (residual.astype(jnp.float32) + attention_sum).astype(jnp.bfloat16)
    normed = layer_norm(hidden_state, norm_gain)
    logits = jnp.dot(normed, router_weight, preferred_element_type=jnp.float32)
    matches = expert_ids[:, :, None] == jnp.arange(experts, dtype=jnp.int32)[None, None, :]
    picked = jnp.sum(jnp.where(matches, logits[:, None, :], 0.0), axis=2)
    scores = jnp.exp(picked)
    route_weight = scores / jnp.sum(scores, axis=1, keepdims=True)
    onehot = matches.astype(jnp.int32)
    present = jnp.sum(onehot, axis=1)
    before = jnp.cumsum(present, axis=0) - present
    slot_rank = jnp.sum(onehot * before[:, None, :], axis=2)
    cell_index = expert_ids * CAP + slot_rank
    cells = cell_index[:, :, None] == jnp.arange(experts * CAP, dtype=jnp.int32)[None, None, :]
    assign = jnp.any(cells, axis=1)
    send_rows = jnp.dot(
        assign.astype(jnp.bfloat16).T, normed, preferred_element_type=jnp.float32
    ).astype(jnp.bfloat16)

    quarter = width // 4
    outgoing = jnp.transpose(send_rows.reshape(experts, CAP, 4, quarter), (0, 2, 1, 3))
    landed = swap(outgoing.reshape(4 * experts, CAP, quarter), EXPERT)
    landed, partner = lax.optimization_barrier((landed, partner))
    block_rows = lax.all_gather(landed.reshape(-1, quarter), "I")

    def turn(value, by):
        return lax.ppermute(value, "Y", [(i, (i + by) % 4) for i in range(4)])

    low, high = block_rows[:2], block_rows[2:]
    below_low, above_high = turn(low, 1), turn(high, -1)
    below_high, above_low = turn(high, 1), turn(low, -1)
    far = [turn(below_low, 1), turn(above_high, -1)]
    near_below, near_above = both_cores(
        [[below_low, below_high], [above_low, above_high]], weights, partner
    )
    *far, near_below, near_above = lax.optimization_barrier((*far, near_below, near_above))
    to_below, to_above = turn(near_below, -1), turn(near_above, 1)
    far_block = over_block(both_cores([far], weights, partner)[0])
    to_far = turn(far_block.astype(jnp.bfloat16), 2)
    own = both_cores([[block_rows]], weights, partner)[0]
    near = own.astype(jnp.float32) + to_below.astype(jnp.float32) + to_above.astype(jnp.float32)
    summed = over_block(near.astype(jnp.bfloat16)) + to_far.astype(jnp.float32)
    back = swap(summed.astype(jnp.bfloat16).reshape(4 * experts, CAP, quarter), EXPERT)
    chosen = jnp.transpose(back.reshape(experts, 4, CAP, quarter), (0, 2, 1, 3))
    chosen = chosen.reshape(experts * CAP, width)
    cell_weight = jnp.sum(jnp.where(cells, route_weight[:, :, None], 0.0), axis=1)
    expert_mix = jnp.dot(
        cell_weight, chosen.astype(jnp.float32), precision=lax.Precision.HIGHEST
    ).astype(jnp.bfloat16)
    return (hidden_state, expert_mix)


def solution(mesh):
    fine = Mesh(np.asarray(mesh.devices).reshape(SIZES), AXES)
    whole = EXPERT + TENSOR
    placed = (
        P(EXPERT, TENSOR),
        P(TENSOR, EXPERT),
        P(whole, None),
        P(),
        P(),
        P(None, whole),
        P(None, whole),
        P(whole, None),
        P(whole, None),
    )
    return jax.shard_map(
        on_device,
        mesh=fine,
        in_specs=placed,
        out_specs=(P(whole, None), P(whole, None)),
        check_vma=False,
    )
```

```python
import functools

import jax
import jax.numpy as jnp
import numpy as np
from jax import lax
from jax.experimental import pallas as pl
from jax.experimental.pallas import tpu as pltpu
from jax.sharding import Mesh, PartitionSpec as P

CAP = 2
AXES = ("X", "B", "I", "Y", "C")
SIZES = (4, 4, 4, 4, 2)
EXPERT = ("X", "B", "I")
TENSOR = ("Y", "C")

norm_epsilon = 1e-05


def layer_norm(state, norm_gain):
    values = state.astype(jnp.float32)
    row_mean = jnp.mean(values, axis=-1, keepdims=True)
    centred = values - row_mean
    variance = jnp.mean(centred * centred, axis=-1, keepdims=True)
    return (centred * lax.rsqrt(variance + norm_epsilon) * norm_gain.astype(jnp.float32)).astype(
        jnp.bfloat16
    )


def swap(value, axes):
    return lax.all_to_all(value, axes, split_axis=0, concat_axis=0, tiled=True)


def spread(value, axes, parts):
    return swap(jnp.broadcast_to(value[None], (parts,) + value.shape), axes)


def attention_rows(context, out_weight, weights, later):
    tokens = spread(context, "X", 4).reshape(-1, context.shape[1])
    columns = lax.all_gather(out_weight.T, ("B", "I"), axis=0, tiled=True)
    partial_sum = lax.dot_general(
        tokens, columns, (((1,), (1,)), ((), ())), preferred_element_type=jnp.float32
    ).astype(jnp.bfloat16)
    partial_sum, weights, later = lax.optimization_barrier((partial_sum, weights, later))
    partner = tuple(lax.ppermute(w, "C", [(0, 1), (1, 0)]) for w in weights)
    width = columns.shape[0]
    pieces = swap(partial_sum.reshape(32, -1, width), ("X", "Y", "C"))
    pieces = pieces.reshape(4, 8, -1, width).astype(jnp.float32)
    summed = jnp.transpose(jnp.sum(pieces, axis=1), (1, 0, 2)).reshape(-1, 4 * width)
    return summed, partner, later


def expert_kernel(layout, *refs):
    pieces = sum(len(group) for group in layout)
    inputs, refs = refs[:pieces], refs[pieces:]
    g0, u0, d0, g1, u1, d1 = refs[:6]
    results, sums = refs[6 : 6 + len(layout)], refs[-1]
    step = results[0].shape[2]
    rows = results[0].shape[1]
    sums[...] = jnp.zeros_like(sums)
    for part in range(results[0].shape[0]):
        at = slice(part * step, (part + 1) * step)
        held = []
        first = 0
        for group in layout:
            left = part
            for number, parts in enumerate(group):
                if 0 <= left < parts:
                    held.append(inputs[first + number][left])
                left -= parts
            first += len(group)
        piece = jnp.concatenate(held, axis=0) if len(held) > 1 else held[0]
        for i, weight in enumerate((g0, u0, g1, u1)):
            sums[i] += jnp.dot(piece, weight[at, :], preferred_element_type=jnp.float32)
    first = (jax.nn.silu(sums[0]) * sums[1]).astype(jnp.bfloat16)
    second = (jax.nn.silu(sums[2]) * sums[3]).astype(jnp.bfloat16)
    for part in range(results[0].shape[0]):
        at = slice(part * step, (part + 1) * step)
        total = jnp.dot(first, d0[:, at], preferred_element_type=jnp.float32)
        total += jnp.dot(second, d1[:, at], preferred_element_type=jnp.float32)
        total = total.astype(jnp.bfloat16)
        for number, result in enumerate(results):
            result[part] = total[number * rows : (number + 1) * rows]


def both_cores(groups, weights, partner):
    layout = tuple(tuple(p.shape[0] for p in group) for group in groups)
    parts, (rows, step) = sum(layout[0]), groups[0][0].shape[1:]
    count, width, units = rows * len(groups), parts * step, weights[0].shape[1]
    vmem = pl.BlockSpec(memory_space=pltpu.VMEM)
    flat = [p for group in groups for p in group]
    return pl.pallas_call(
        functools.partial(expert_kernel, layout),
        out_shape=[jax.ShapeDtypeStruct((parts, rows, step), jnp.bfloat16)] * len(groups),
        in_specs=[vmem] * (len(flat) + 6),
        out_specs=[vmem] * len(groups),
        scratch_shapes=[pltpu.VMEM((4, count, units), jnp.float32)],
        compiler_params=pltpu.CompilerParams(vmem_limit_bytes=32 * 1024 * 1024),
        cost_estimate=pl.CostEstimate(
            flops=12 * count * width * units,
            bytes_accessed=4 * count * width + 12 * width * units,
            transcendentals=2 * count * units,
        ),
    )(*flat, *weights, *partner)


def over_block(value):
    return jnp.sum(swap(value, "I").astype(jnp.float32), axis=0)


def on_device(
    context,
    out_weight,
    residual,
    norm_gain,
    router_weight,
    gate_weight,
    up_weight,
    down_weight,
    expert_ids,
):
    width = residual.shape[1]
    experts = router_weight.shape[1]
    weights = (gate_weight, up_weight, down_weight)
    attention_sum, partner, (expert_ids, norm_gain) = attention_rows(
        context, out_weight, weights, (expert_ids, norm_gain)
    )
    hidden_state = (residual.astype(jnp.float32) + attention_sum).astype(jnp.bfloat16)
    normed = layer_norm(hidden_state, norm_gain)
    logits = jnp.dot(normed, router_weight, preferred_element_type=jnp.float32)
    matches = expert_ids[:, :, None] == jnp.arange(experts, dtype=jnp.int32)[None, None, :]
    picked = jnp.sum(jnp.where(matches, logits[:, None, :], 0.0), axis=2)
    scores = jnp.exp(picked)
    route_weight = scores / jnp.sum(scores, axis=1, keepdims=True)
    onehot = matches.astype(jnp.int32)
    present = jnp.sum(onehot, axis=1)
    before = jnp.cumsum(present, axis=0) - present
    slot_rank = jnp.sum(onehot * before[:, None, :], axis=2)
    cell_index = expert_ids * CAP + slot_rank
    cells = cell_index[:, :, None] == jnp.arange(experts * CAP, dtype=jnp.int32)[None, None, :]
    assign = jnp.any(cells, axis=1)
    send_rows = jnp.dot(
        assign.astype(jnp.bfloat16).T, normed, preferred_element_type=jnp.float32
    ).astype(jnp.bfloat16)

    quarter = width // 4
    outgoing = jnp.transpose(send_rows.reshape(experts, CAP, 4, quarter), (0, 2, 1, 3))
    landed = swap(outgoing.reshape(4 * experts, CAP, quarter), EXPERT)
    landed, partner = lax.optimization_barrier((landed, partner))
    block_rows = lax.all_gather(landed.reshape(-1, quarter), "I")

    def turn(value, by):
        return lax.ppermute(value, "Y", [(i, (i + by) % 4) for i in range(4)])

    low, high = block_rows[:2], block_rows[2:]
    below_low, above_high = turn(low, 1), turn(high, -1)
    below_high, above_low = turn(high, 1), turn(low, -1)
    far = [turn(below_low, 1), turn(above_high, -1)]
    near_below, near_above = both_cores(
        [[below_low, below_high], [above_low, above_high]], weights, partner
    )
    *far, near_below = lax.optimization_barrier((*far, near_below))
    to_below, to_above = turn(near_below, -1), turn(near_above, 1)
    far_block = over_block(both_cores([far], weights, partner)[0])
    to_far = turn(far_block.astype(jnp.bfloat16), 2)
    own = both_cores([[block_rows]], weights, partner)[0]
    near = own.astype(jnp.float32) + to_below.astype(jnp.float32) + to_above.astype(jnp.float32)
    summed = over_block(near.astype(jnp.bfloat16)) + to_far.astype(jnp.float32)
    back = swap(summed.astype(jnp.bfloat16).reshape(4 * experts, CAP, quarter), EXPERT)
    chosen = jnp.transpose(back.reshape(experts, 4, CAP, quarter), (0, 2, 1, 3))
    chosen = chosen.reshape(experts * CAP, width)
    cell_weight = jnp.sum(jnp.where(cells, route_weight[:, :, None], 0.0), axis=1)
    expert_mix = jnp.dot(
        cell_weight, chosen.astype(jnp.float32), precision=lax.Precision.HIGHEST
    ).astype(jnp.bfloat16)
    return (hidden_state, expert_mix)


def solution(mesh):
    fine = Mesh(np.asarray(mesh.devices).reshape(SIZES), AXES)
    whole = EXPERT + TENSOR
    placed = (
        P(EXPERT, TENSOR),
        P(TENSOR, EXPERT),
        P(whole, None),
        P(),
        P(),
        P(None, whole),
        P(None, whole),
        P(whole, None),
        P(whole, None),
    )
    return jax.shard_map(
        on_device,
        mesh=fine,
        in_specs=placed,
        out_specs=(P(whole, None), P(whole, None)),
        check_vma=False,
    )
```
